1024 devices in a mesh: rows: 64 (over y, z), cols: 16 (over x, core).
Axes of the slice: x: 8, y: 8, z: 8, core: 2. Of those that a mesh axis runs over, the one named last changes fastest.
Arguments:
- hamiltonian: float32 [256, 8, 128, 128], P('rows'), may hold values from -6 to 6
- intersection_root: float32 [256, 8, 128, 128], P('rows'), may hold values from -0.1875 to 0.1875
- ham_pattern: int32 [256, 8], replicated, may hold values from -1 to 255, as said below
- root_pattern: int32 [256, 8], replicated, may hold values from -1 to 255, as said below
- filter_pattern: int32 [256, 8], replicated, may hold values from -1 to 255, as said below
Outputs:
- projected: float32 [256, 8, 128, 128], P('rows', None, 'cols')
The draws below stay inside these ranges and needn't reach their ends.
Inputs may be any that keep to these rules, and one draw needn't show every extreme that they name: `ham_pattern`: in every row i the used slots come first and hold distinct block columns, all within 4 block rows of i counted cyclically over the 256 block rows; slot 0 holds i itself; every row uses 2 or more slots and some row uses all 8. `root_pattern`: same rules as ham_pattern, drawn independently. `filter_pattern`: same rules as ham_pattern, drawn independently.
All inputs are finite; a program needn't handle non-finite values.
Results may differ from the reference program's by a relative error of at most 0.0003.
Values sent between devices are 32-bit elements; how exact they have to be, the bound alone decides.
A program may use at most 32 MiB of HBM per device.

```python
import jax
import jax.numpy as jnp
from jax import lax

B = 128
KC = 8
REACH = 4
BLOCK_ROWS = 256


def pattern_draw(key, salt):
    key = jax.random.fold_in(key, salt)
    count_key, order_key = jax.random.split(key)
    span_width = 2 * REACH + 1
    block_scores = jax.random.randint(order_key, (BLOCK_ROWS, span_width), 0, 1 << 20) * span_width
    block_scores = block_scores + jnp.arange(span_width, dtype=jnp.int32)[None, :]
    block_scores = block_scores.at[:, REACH].set(-1)
    ordering = jnp.argsort(block_scores, axis=1, stable=True)[:, :KC].astype(jnp.int32)
    offsets = ordering - REACH
    row_ids = jnp.arange(BLOCK_ROWS, dtype=jnp.int32)
    block_counts = jax.random.randint(count_key, (BLOCK_ROWS,), 2, KC + 1)
    block_counts = jnp.where(row_ids % 5 == 0, KC, block_counts)
    columns = jnp.mod(row_ids[:, None] + offsets, BLOCK_ROWS)
    slot_ids = jnp.arange(KC, dtype=jnp.int32)[None, :]
    return jnp.where(slot_ids < block_counts[:, None], columns, -1).astype(jnp.int32)


def draw_ham_pattern(key, part):
    return pattern_draw(key, 11)


def draw_root_pattern(key, part):
    return pattern_draw(key, 23)


def draw_filter_pattern(key, part):
    return pattern_draw(key, 37)


def block_levels(key, dims, shards, least, largest):
    level, own = 1.0, jax.random.fold_in(key, 6)
    for dim, shards_of in shards:
        steps = jnp.exp(jax.random.uniform(jax.random.fold_in(own, dim), (shards_of,), jnp.float32, least / len(shards), largest / len(shards)))
        level = level * jnp.repeat(steps, dims[dim] // shards_of).reshape([-1 if axis == dim else 1 for axis in range(len(dims))])
    return level


def bell_draw(rng, extent, width, bound, cuts=(), held_as=jnp.bfloat16):
    level = block_levels(rng, extent, cuts, -0.22, 0.18) if cuts else 1.0
    drawn = jax.random.normal(rng, extent, jnp.float32) * width * level
    return jnp.minimum(jnp.maximum(drawn, -bound), bound).astype(held_as)


def setup_inputs(seed: int = 0) -> dict:
    key_of = jax.random.split(jax.random.key(seed), 6)
    hamiltonian = bell_draw(key_of[0], (BLOCK_ROWS, KC, B, B), 1.0, 6.0, ((0, 64),), jnp.float32)
    intersection_root = bell_draw(key_of[1], (BLOCK_ROWS, KC, B, B), (B * KC) ** -0.5, 0.1875, ((0, 64),), jnp.float32)
    ham_pattern = draw_ham_pattern(jax.random.fold_in(key_of[5], 71), 0)
    root_pattern = draw_root_pattern(jax.random.fold_in(key_of[5], 71), 0)
    filter_pattern = draw_filter_pattern(jax.random.fold_in(key_of[5], 71), 0)
    return dict(hamiltonian=hamiltonian, intersection_root=intersection_root, ham_pattern=ham_pattern, root_pattern=root_pattern, filter_pattern=filter_pattern)


HIGHEST_ACCURACY = lax.Precision.HIGHEST


def filtered_product(left_blocks, left_columns, right_blocks, right_columns, out_columns):
    def one_row(row_data):
        block_list, columns, kept_columns = row_data
        usable = columns >= 0
        safe_columns = jnp.where(usable, columns, 0)
        picked = right_blocks[safe_columns]
        matches = (right_columns[safe_columns][:, :, None] == kept_columns[None, None, :]) & (kept_columns[None, None, :] >= 0) & usable[:, None, None]
        selected_blocks = jnp.einsum("sut,subc->stbc", matches.astype(jnp.float32), picked, precision=HIGHEST_ACCURACY)
        return jnp.einsum("lyj,ldjr->dyr", block_list, selected_blocks, precision=HIGHEST_ACCURACY)

    return lax.map(one_row, (left_blocks, left_columns, out_columns))


def congruence(root_blocks, root_columns, product, product_columns):
    total_rows = root_blocks.shape[0]
    offsets = jnp.arange(-REACH, REACH + 1, dtype=jnp.int32)

    def one_row(row_data):
        row_index, kept_columns = row_data
        nearby = jnp.mod(row_index + offsets, total_rows).astype(jnp.int32)
        matched = (root_columns[nearby] == row_index).astype(jnp.float32)
        fetched_blocks = jnp.einsum("ds,dsba->dba", matched, root_blocks[nearby], precision=HIGHEST_ACCURACY)
        matches = (product_columns[nearby][:, :, None] == kept_columns[None, None, :]) & (kept_columns[None, None, :] >= 0)
        selected_blocks = jnp.einsum("dut,dubc->dtbc", matches.astype(jnp.float32), product[nearby], precision=HIGHEST_ACCURACY)
        return jnp.einsum("nuw,niuy->iwy", fetched_blocks, selected_blocks, precision=HIGHEST_ACCURACY)

    return lax.map(one_row, (jnp.arange(total_rows, dtype=jnp.int32), product_columns))


def reference(hamiltonian, intersection_root, ham_pattern, root_pattern, filter_pattern):
    product = filtered_product(hamiltonian, ham_pattern, intersection_root, root_pattern, filter_pattern)
    density = congruence(intersection_root, root_pattern, product, filter_pattern)
    square = filtered_product(density, filter_pattern, density, filter_pattern, filter_pattern)
    purified = 2.0 * density - square
    projected = filtered_product(intersection_root, root_pattern, purified, filter_pattern, filter_pattern)
    return jnp.swapaxes(projected, 2, 3)
```

```python
import functools

import jax
import jax.numpy as jnp
from jax import lax
from jax.experimental import pallas as pl
from jax.experimental.pallas import tpu as pltpu
from jax.sharding import PartitionSpec as P

R = 4
K = 8
N = 128
C = 8
BAND = 2 * R + 1
WIN = 3 * R
CHIPS = 8
F32, BF16 = jnp.float32, jnp.bfloat16


def split(x):
    hi = x.astype(BF16).astype(F32)
    return hi, x - hi


def stacked(x):
    return jnp.concatenate(split(x), 0).astype(BF16)


def rows_of(tiles):
    return tiles.reshape(tiles.shape[0] * C, N)


def quadrants(x):
    half = x.shape[0] // 2
    return (x[half:, N:] + x[half:, :N]) + (x[:half, N:] + x[:half, :N])


def dot(a, b, b_dim):
    return lax.dot_general(a, b, (((1,), (b_dim,)), ((), ())), preferred_element_type=F32)


def kernel(
    total_rows, h_hbm, z_hbm, hp_hbm, rp_hbm, fp_hbm, out,
    hp, rp, fp, zbuf, hbuf, hsplit, zsplit, merged, zslot, zwin, wband, part, from_next, from_prev,
    xwin, xband, xall, lefts, pwin, yband,
    load_sem, pat_sem, halo_send, halo_recv, part_send, part_recv, ring_send, ring_recv, pair_send, pair_recv,
):
    groups = total_rows // R
    row, col = lax.axis_index("rows"), lax.axis_index("cols")
    chip, core = col // 2, lax.rem(col, 2)
    first = row * R
    nxt = {"rows": lax.rem(row + 1, groups), "cols": col}
    prv = {"rows": lax.rem(row + groups - 1, groups), "cols": col}
    right = {"rows": row, "cols": lax.rem(chip + 1, CHIPS) * 2 + core}
    left = {"rows": row, "cols": lax.rem(chip + CHIPS - 1, CHIPS) * 2 + core}
    other = {"rows": row, "cols": chip * 2 + (1 - core)}

    pats = [
        pltpu.make_async_copy(a, b, pat_sem.at[i])
        for i, (a, b) in enumerate(((rp_hbm, rp), (hp_hbm, hp), (fp_hbm, fp)))
    ]
    zloads = [pltpu.make_async_copy(z_hbm.at[k], zbuf.at[k], load_sem.at[0, k]) for k in range(R)]
    hloads = [pltpu.make_async_copy(h_hbm.at[k], hbuf.at[k], load_sem.at[1, k]) for k in range(R)]
    for c in pats + zloads + hloads:
        c.start()

    with jax.named_scope("zeros"):
        for win in (zwin, xwin, pwin):
            for r in range(WIN + 1):
                win[r] = jnp.zeros((WIN + 1, C, N), F32)
        for k in range(R):
            wband[k] = jnp.zeros((WIN, C, N), F32)
            yband[k] = jnp.zeros((WIN + 1, C, N), F32)
            xband[k, WIN] = jnp.zeros((C, N), F32)
            zslot[k, K] = jnp.zeros((C, N), F32)
            zsplit[k, K] = jnp.zeros((N, 2 * N), BF16)

    barrier = pltpu.get_barrier_semaphore()
    for device in (nxt, prv, right, left, other):
        pl.semaphore_signal(barrier, inc=1, device_id=device, device_id_type=pl.DeviceIdType.MESH)

    for c in pats:
        c.wait()

    def relative(pat, i, s):
        p = pat[s, first + i]
        v = p - first + R
        v = jnp.where(v < 0, v + total_rows, v)
        v = jnp.where(v >= total_rows, v - total_rows, v)
        return jnp.where(p < 0, WIN, jnp.minimum(v, WIN))

    def slot_at(rel, i, d):
        slot = jnp.int32(K)
        for s in range(K):
            slot = jnp.where(rel[i][s] == i + d, s, slot)
        return slot

    with jax.named_scope("root tables"):
        rrel = [[relative(rp, i, s) for s in range(K)] for i in range(R)]
        zslots = [[slot_at(rrel, i, d) for d in range(BAND)] for i in range(R)]

    lane = lax.broadcasted_iota(jnp.int32, (N, N), 1) // C
    with jax.named_scope("columns of Z"):
        for pair in range(R // 2):
            for k in (2 * pair, 2 * pair + 1):
                zloads[k].wait()
            m = jnp.zeros((N, N), F32)
            for q in range(2 * K):
                v = zbuf[2 * pair + q // K, q % K]
                v = jnp.where(lane == col, v, 0.0)
                m += pltpu.roll(v, q * C, 1) if q else v
            merged[pair] = m.T
            for q in range(2 * K):
                at = pl.multiple_of(lax.rem(col + q, 2 * K) * C, C)
                zslot[2 * pair + q // K, q % K] = merged[pair, pl.ds(at, C), :]
        for k in range(R):
            for d in range(BAND):
                zwin[R + k, k + d] = zslot[k, zslots[k][d]]

    with jax.named_scope("entry wait"):
        pl.semaphore_wait(barrier, 5)

    def copy(src, dst, send, recv, device):
        return pltpu.make_async_remote_copy(
            src_ref=src, dst_ref=dst, send_sem=send, recv_sem=recv, device_id=device,
            device_id_type=pl.DeviceIdType.MESH,
        )

    def halo(win, stage, r):
        up = copy(
            win.at[R + r, pl.ds(R, r + R + 1)], win.at[r, pl.ds(0, r + R + 1)],
            halo_send.at[stage, 0, r], halo_recv.at[stage, 0, r], nxt,
        )
        down = copy(
            win.at[R + r, pl.ds(r, 2 * R - r)], win.at[2 * R + r, pl.ds(r + R, 2 * R - r)],
            halo_send.at[stage, 1, r], halo_recv.at[stage, 1, r], prv,
        )
        return up, down

    halos = [[halo(win, stage, r) for r in range(R)] for stage, win in enumerate((zwin, xwin, pwin))]
    for r in range(R):
        for c in halos[0][r]:
            c.start()

    with jax.named_scope("other tables"):
        hrel = [[relative(hp, i, s) for s in range(K)] for i in range(R)]
        frel = [[relative(fp, i, s) for s in range(K)] for i in range(R)]
        keep = [[(slot_at(frel, i, d) < K).astype(F32) for d in range(BAND)] for i in range(R)]

    with jax.named_scope("parts of H and Z"):
        for k in range(R):
            for s in range(K):
                hi, lo = split(zbuf[k, s])
                zsplit[k, s] = jnp.concatenate([hi, lo], 1).astype(BF16)
        for k in range(R):
            hloads[k].wait()
            for s in range(K):
                hsplit[k, s] = stacked(hbuf[k, s])

    with jax.named_scope("halo of Z wait"):
        for r in range(R):
            for c in halos[0][r]:
                c.wait_recv()

    with jax.named_scope("product W"):
        for i in range(R):
            lhs = jnp.concatenate([stacked(rows_of(zwin[hrel[i][s], i : i + BAND])) for s in range(K)], 1)
            rhs = jnp.concatenate([hsplit[i, s] for s in range(K)], 1)
            w = quadrants(dot(lhs, rhs, 1))
            for d in range(BAND):
                wband[i, i + d] = w[C * d : C * d + C] * keep[i][d]

    def part_copy(w):
        if w < R:
            n = w + R + 1
            return copy(
                part.at[w, pl.ds(0, n)], from_next.at[w, pl.ds(R, n)], part_send.at[w], part_recv.at[w], prv
            )
        r = w - 2 * R
        n = 2 * R - r
        return copy(
            part.at[w, pl.ds(r + R, n)], from_prev.at[r, pl.ds(r, n)], part_send.at[r + R], part_recv.at[r + R], nxt
        )

    parts = {w: part_copy(w) for w in (*range(R), *range(2 * R, 3 * R))}
    order = [w for r in range(R) for w in (r, 2 * R + r)] + list(range(R, 2 * R))
    with jax.named_scope("partial X"):
        for w in order:
            ks = [k for k in range(R) if 0 <= w - k < BAND]
            lo, hi = max(0, w - R), min(WIN, w + R + 1)
            lhs = jnp.concatenate([stacked(rows_of(wband[k, lo:hi])) for k in ks], 1)
            rhs = jnp.concatenate([zsplit[k, zslots[k][w - k]] for k in ks], 0)
            x = quadrants(dot(lhs, rhs, 0))
            for j in range(lo, hi):
                part[w, j] = x[C * (j - lo) : C * (j - lo) + C]
            if w in parts:
                parts[w].start()

    def shard(chip_, core_, i):
        return xall.at[i, :, pl.ds(pl.multiple_of((chip_ * 2 + core_) * C, C), C), :]

    def ring(direction, dist, i):
        device = right if direction == 0 else left
        source = lax.rem(chip + (1 - dist if direction == 0 else dist - 1) + CHIPS, CHIPS)
        ref = shard(source, core, i)
        return copy(ref, ref, ring_send.at[direction, dist - 1, i], ring_recv.at[direction, dist - 1, i], device)

    def landed(direction, dist, i):
        source = lax.rem(chip + (-dist if direction == 0 else dist) + CHIPS, CHIPS)
        ref = shard(source, core, i)
        return copy(
            ref, ref, ring_send.at[direction, dist - 1, i], ring_recv.at[direction, dist - 1, i],
            right if direction == 0 else left,
        )

    def pair(offset, i, mine):
        source = lax.rem(chip + offset, CHIPS)
        ref = shard(source, core if mine else 1 - core, i)
        return copy(ref, ref, pair_send.at[offset, i], pair_recv.at[offset, i], other)

    sent = []

    def start(c):
        c.start()
        sent.append(c)

    with jax.named_scope("sum X"):
        for i in range(R):
            parts[i].wait_recv()
            parts[2 * R + i].wait_recv()
            for d in range(BAND):
                j = i + d
                x = part[R + i, j]
                if j >= R:
                    x += from_next[i, j]
                if j < 2 * R:
                    x += from_prev[i, j]
                x *= keep[i][d]
                xwin[R + i, j] = x
                xband[i, j] = x
            at = pl.ds(pl.multiple_of(col * C, C), C)
            for t in range(K):
                xall[i, t, at, :] = xband[i, frel[i][t]]
            start(ring(0, 1, i))
            start(ring(1, 1, i))
            start(pair(0, i, True))
            for c in halos[1][i]:
                c.start()

    far = CHIPS // 2

    def steps(i, dist):
        for direction in (0, 1):
            if dist == far and i % 2 != direction:
                continue
            landed(direction, dist, i).wait_recv()
            if dist < far - 1 or (dist == far - 1 and i % 2 == direction):
                start(ring(direction, dist + 1, i))
            start(pair(CHIPS - dist if direction == 0 else dist, i, True))

    with jax.named_scope("step 1"):
        for i in range(R):
            steps(i, 1)

    with jax.named_scope("halo of X wait"):
        for r in range(R):
            for c in halos[1][r]:
                c.wait_recv()

    with jax.named_scope("step 2"):
        for i in range(R):
            steps(i, 2)
            lefts[i] = jnp.concatenate([stacked(rows_of(xwin[frel[i][s], i : i + BAND])) for s in range(K)], 1)

    with jax.named_scope("step 3"):
        for i in range(R):
            steps(i, 3)

    with jax.named_scope("step 4 and product S"):
        for i in range(R):
            steps(i, 4)
            for offset in range(CHIPS):
                pair(offset, i, False).wait_recv()
            rhs = []
            for s in range(K):
                hi, lo = split(xall[i, s])
                rhs.append(jnp.concatenate([hi, lo], 1).astype(BF16))
            square = quadrants(dot(lefts[i], jnp.concatenate(rhs, 0), 0))
            for d in range(BAND):
                pwin[R + i, i + d] = 2.0 * xwin[R + i, i + d] - square[C * d : C * d + C] * keep[i][d]
            for c in halos[2][i]:
                c.start()

    with jax.named_scope("halo of P wait"):
        for r in range(R):
            for c in halos[2][r]:
                c.wait_recv()

    with jax.named_scope("product Y"):
        for i in range(R):
            lhs = jnp.concatenate([stacked(rows_of(pwin[rrel[i][s], i : i + BAND])) for s in range(K)], 1)
            rhs = jnp.concatenate(
                [jnp.concatenate([zsplit[i, s, :, :N], zsplit[i, s, :, N:]], 0) for s in range(K)], 1
            )
            y = quadrants(dot(lhs, rhs, 1))
            for d in range(BAND):
                yband[i, i + d] = y[C * d : C * d + C]
            for t in range(K):
                out[i, t] = yband[i, frel[i][t]]

    with jax.named_scope("drain"):
        for stage in range(3):
            for r in range(R):
                for c in halos[stage][r]:
                    c.wait_send()
        for c in parts.values():
            c.wait_send()
        for c in sent:
            c.wait_send()

def shards(hamiltonian, intersection_root, ham_pattern, root_pattern, filter_pattern):

    total_rows = ham_pattern.shape[0]
    hbm = pl.BlockSpec(memory_space=pltpu.HBM)
    dma = pltpu.SemaphoreType.DMA
    window = pltpu.VMEM((WIN + 1, WIN + 1, C, N), F32)
    return pl.pallas_call(
        functools.partial(kernel, total_rows),
        out_shape=jax.ShapeDtypeStruct((R, K, C, N), F32),
        in_specs=[hbm] * 5,
        out_specs=pl.BlockSpec(memory_space=pltpu.VMEM),
        scratch_shapes=[
            *[pltpu.SMEM((K, total_rows), jnp.int32)] * 3,
            pltpu.VMEM((R, K, N, N), F32),
            pltpu.VMEM((R, K, N, N), F32),
            pltpu.VMEM((R, K, 2 * N, N), BF16),
            pltpu.VMEM((R, K + 1, N, 2 * N), BF16),
            pltpu.VMEM((R // 2, N, N), F32),
            pltpu.VMEM((R, K + 1, C, N), F32),
            window,
            pltpu.VMEM((R, WIN, C, N), F32),
            pltpu.VMEM((WIN, WIN, C, N), F32),
            pltpu.VMEM((R, WIN, C, N), F32),
            pltpu.VMEM((R, WIN, C, N), F32),
            window,
            pltpu.VMEM((R, WIN + 1, C, N), F32),
            pltpu.VMEM((R, K, N, N), F32),
            pltpu.VMEM((R, 2 * BAND * C, K * N), BF16),
            window,
            pltpu.VMEM((R, WIN + 1, C, N), F32),
            dma((2, R)),
            dma((3,)),
            dma((3, 2, R)),
            dma((3, 2, R)),
            dma((2 * R,)),
            dma((2 * R,)),
            dma((2, CHIPS // 2, R)),
            dma((2, CHIPS // 2, R)),
            dma((CHIPS, R)),
            dma((CHIPS, R)),
        ],
        compiler_params=pltpu.CompilerParams(
            collective_id=0, has_side_effects=True, vmem_limit_bytes=63 * 2**20
        ),
        cost_estimate=pl.CostEstimate(flops=4 * 270_000_000, bytes_accessed=4_400_000, transcendentals=0),
    )(hamiltonian, intersection_root, ham_pattern.T, root_pattern.T, filter_pattern.T)


def solution(mesh):
    return jax.shard_map(
        shards,
        mesh=mesh,
        in_specs=(P("rows", None, None, None), P("rows", None, None, None), P(), P(), P()),
        out_specs=P("rows", None, "cols", None),
        check_vma=False,
    )
```

```python
import functools

import jax
import jax.numpy as jnp
from jax import lax
from jax.experimental import pallas as pl
from jax.experimental.pallas import tpu as pltpu
from jax.sharding import PartitionSpec as P

R = 4
K = 8
N = 128
C = 8
BAND = 2 * R + 1
WIN = 3 * R
CHIPS = 8
HALF = R // 2
F32, BF16 = jnp.float32, jnp.bfloat16


def split(x):
    hi = x.astype(BF16).astype(F32)
    return hi, x - hi


def stacked(x):
    return jnp.concatenate(split(x), 0).astype(BF16)


def rows_of(tiles):
    return tiles.reshape(tiles.shape[0] * C, N)


def quadrants(x):
    half = x.shape[0] // 2
    return (x[half:, N:] + x[half:, :N]) + (x[:half, N:] + x[:half, :N])


def dot(a, b, b_dim):
    return lax.dot_general(a, b, (((1,), (b_dim,)), ((), ())), preferred_element_type=F32)


def kernel(
    total_rows, h_hbm, z_hbm, hp_hbm, rp_hbm, fp_hbm, out,
    hp, rp, fp, zbuf, hbuf, hsplit, zsplit, merged, zslot, zwin, wband, part, from_next, from_prev,
    xwin, xwin_other, xband, xslot, xall, lefts, pwin, pother, yband,
    load_sem, pat_sem, halo_send, halo_recv, part_send, part_recv, ring_send, ring_recv,
    give_send, give_recv, own_send, own_recv, pass_send, pass_recv, p_send, p_recv, p_give_recv,
):
    groups = total_rows // R
    row, col = lax.axis_index("rows"), lax.axis_index("cols")
    chip, core = col // 2, lax.rem(col, 2)
    mate = chip * 2 + (1 - core)
    first = row * R
    up, down = lax.rem(row + 1, groups), lax.rem(row + groups - 1, groups)
    nxt, prv = {"rows": up, "cols": col}, {"rows": down, "cols": col}
    nxt_other, prv_other = {"rows": up, "cols": mate}, {"rows": down, "cols": mate}
    right = {"rows": row, "cols": lax.rem(chip + 1, CHIPS) * 2 + core}
    left = {"rows": row, "cols": lax.rem(chip + CHIPS - 1, CHIPS) * 2 + core}
    other = {"rows": row, "cols": mate}

    pats = [
        pltpu.make_async_copy(a, b, pat_sem.at[i])
        for i, (a, b) in enumerate(((rp_hbm, rp), (hp_hbm, hp), (fp_hbm, fp)))
    ]
    zloads = [pltpu.make_async_copy(z_hbm.at[k], zbuf.at[k], load_sem.at[0, k]) for k in range(R)]
    hloads = [pltpu.make_async_copy(h_hbm.at[k], hbuf.at[k], load_sem.at[1, k]) for k in range(R)]
    for c in pats + zloads + hloads:
        c.start()

    for win in (zwin, xwin, xwin_other, pwin):
        for r in range(WIN + 1):
            win[r] = jnp.zeros((WIN + 1, C, N), F32)
    for k in range(R):
        wband[k] = jnp.zeros((WIN, C, N), F32)
        yband[k] = jnp.zeros((WIN + 1, C, N), F32)
        xband[k, WIN] = jnp.zeros((C, N), F32)
        zslot[k, K] = jnp.zeros((C, N), F32)
        zsplit[k, K] = jnp.zeros((N, 2 * N), BF16)
    for r in range(HALF):
        pother[r] = jnp.zeros((WIN, C, N), F32)

    barrier = pltpu.get_barrier_semaphore()
    neighbours = (nxt, prv, right, left, other, nxt_other, prv_other)
    for device in neighbours:
        pl.semaphore_signal(barrier, inc=1, device_id=device, device_id_type=pl.DeviceIdType.MESH)

    for c in pats:
        c.wait()

    def relative(pat, i, s):
        p = pat[s, first + i]
        v = p - first + R
        v = jnp.where(v < 0, v + total_rows, v)
        v = jnp.where(v >= total_rows, v - total_rows, v)
        return jnp.where(p < 0, WIN, jnp.minimum(v, WIN))

    def slot_at(rel, i, d):
        slot = jnp.int32(K)
        for s in range(K):
            slot = jnp.where(rel[s] == i + d, s, slot)
        return slot

    def kept(rel, i):
        return [(slot_at(rel, i, d) < K).astype(F32) for d in range(BAND)]

    rrel = [[relative(rp, i, s) for s in range(K)] for i in range(R)]
    zslots = [[slot_at(rrel[i], i, d) for d in range(BAND)] for i in range(R)]

    def copy(src, dst, send, recv, device):
        return pltpu.make_async_remote_copy(
            src_ref=src, dst_ref=dst, send_sem=send, recv_sem=recv, device_id=device,
            device_id_type=pl.DeviceIdType.MESH,
        )

    sent = []

    def start(c):
        c.start()
        sent.append(c)

    def halo(win, stage, r):
        ahead = copy(
            win.at[R + r, pl.ds(R, r + R + 1)], win.at[r, pl.ds(0, r + R + 1)],
            halo_send.at[stage, 0, r], halo_recv.at[stage, 0, r], nxt,
        )
        back = copy(
            win.at[R + r, pl.ds(r, 2 * R - r)], win.at[2 * R + r, pl.ds(r + R, 2 * R - r)],
            halo_send.at[stage, 1, r], halo_recv.at[stage, 1, r], prv,
        )
        return ahead, back

    halos = [[halo(win, stage, r) for r in range(R)] for stage, win in enumerate((zwin, xwin))]

    lane = lax.broadcasted_iota(jnp.int32, (N, N), 1) // C
    for pair in range(R // 2):
        rows = (2 * pair, 2 * pair + 1)
        for k in rows:
            zloads[k].wait()
        m = jnp.zeros((N, N), F32)
        for q in range(2 * K):
            v = zbuf[2 * pair + q // K, q % K]
            v = jnp.where(lane == col, v, 0.0)
            m += pltpu.roll(v, q * C, 1) if q else v
        merged[pair] = m.T
        for q in range(2 * K):
            at = pl.multiple_of(lax.rem(col + q, 2 * K) * C, C)
            zslot[2 * pair + q // K, q % K] = merged[pair, pl.ds(at, C), :]
        for k in rows:
            for d in range(BAND):
                zwin[R + k, k + d] = zslot[k, zslots[k][d]]
        if pair == 0:
            pl.semaphore_wait(barrier, len(neighbours))
        for k in rows:
            for c in halos[0][k]:
                start(c)

    hrel = [[relative(hp, i, s) for s in range(K)] for i in range(R)]
    frel = [[relative(fp, i, s) for s in range(K)] for i in range(R)]
    keep = [kept(frel[i], i) for i in range(R)]
    mine = [core * HALF + r for r in range(HALF)]
    mine_rel = [[relative(fp, i, s) for s in range(K)] for i in mine]
    mine_keep = [kept(rel, i) for rel, i in zip(mine_rel, mine)]
    for k in range(R):
        for s in range(K):
            hi, lo = split(zbuf[k, s])
            zsplit[k, s] = jnp.concatenate([hi, lo], 1).astype(BF16)
    for k in range(R):
        hloads[k].wait()
        for s in range(K):
            hsplit[k, s] = stacked(hbuf[k, s])
    for r in range(R):
        for c in halos[0][r]:
            c.wait_recv()

    for i in range(R):
        lhs = jnp.concatenate([stacked(rows_of(zwin[hrel[i][s], i : i + BAND])) for s in range(K)], 1)
        rhs = jnp.concatenate([hsplit[i, s] for s in range(K)], 1)
        w = quadrants(dot(lhs, rhs, 1))
        for d in range(BAND):
            wband[i, i + d] = w[C * d : C * d + C] * keep[i][d]

    def part_copy(w):
        if w < R:
            n = w + R + 1
            return copy(
                part.at[w, pl.ds(0, n)], from_next.at[w, pl.ds(R, n)], part_send.at[w], part_recv.at[w], prv
            )
        r = w - 2 * R
        n = 2 * R - r
        return copy(
            part.at[w, pl.ds(r + R, n)], from_prev.at[r, pl.ds(r, n)], part_send.at[r + R], part_recv.at[r + R], nxt
        )

    parts = {w: part_copy(w) for w in (*range(R), *range(2 * R, 3 * R))}
    order = [w for r in range(R) for w in (r, 2 * R + r)] + list(range(R, 2 * R))
    for w in order:
        ks = [k for k in range(R) if 0 <= w - k < BAND]
        lo, hi = max(0, w - R), min(WIN, w + R + 1)
        lhs = jnp.concatenate([stacked(rows_of(wband[k, lo:hi])) for k in ks], 1)
        rhs = jnp.concatenate([zsplit[k, zslots[k][w - k]] for k in ks], 0)
        x = quadrants(dot(lhs, rhs, 0))
        for j in range(lo, hi):
            part[w, j] = x[C * (j - lo) : C * (j - lo) + C]
        if w in parts:
            start(parts[w])

    def ring(direction, dist, r, theirs, source, src=None):
        ref = xall.at[r, source * 2 + (1 - core if theirs else core)]
        piece = 2 * r + theirs
        return copy(
            ref if src is None else src, ref, ring_send.at[direction, dist - 1, piece],
            ring_recv.at[direction, dist - 1, piece], left if direction else right,
        )

    def give(r):
        return copy(xslot.at[(1 - core) * HALF + r], xall.at[r, col], give_send.at[r], give_recv.at[r], other)

    def given(r):
        return copy(xslot.at[r], xall.at[r, mate], give_send.at[r], give_recv.at[r], other)

    for i in range(R):
        parts[i].wait_recv()
        parts[2 * R + i].wait_recv()
        for d in range(BAND):
            j = i + d
            x = part[R + i, j]
            if j >= R:
                x += from_next[i, j]
            if j < 2 * R:
                x += from_prev[i, j]
            x *= keep[i][d]
            xwin[R + i, j] = x
            xband[i, j] = x
        for t in range(K):
            xslot[i, t] = xband[i, frel[i][t]]

        @pl.when(core == i // HALF)
        def _():
            for direction in (0, 1):
                ring(direction, 1, i % HALF, 0, chip, xslot.at[i]).start()

        @pl.when(core != i // HALF)
        def _():
            give(i % HALF).start()

        if i % HALF == HALF - 1 and i > HALF:
            for r in range(HALF):
                given(r).wait_recv()
                for direction in (0, 1):
                    start(ring(direction, 1, r, 1, chip))

    for r in range(HALF):
        sent += [give(r)] + [ring(direction, 1, r, 0, chip, xslot.at[r]) for direction in (0, 1)]

    def own_row(i):
        ref = (R + i, pl.ds(i, BAND))
        return copy(xwin.at[ref], xwin_other.at[ref], own_send.at[i], own_recv.at[i], other)

    def pass_on(direction, r):
        ref = (r, pl.ds(0, r + R + 1)) if direction == 0 else (2 * R + r, pl.ds(r + R, 2 * R - r))
        return copy(xwin.at[ref], xwin_other.at[ref], pass_send.at[direction, r], pass_recv.at[direction, r], other)

    for i in range(R):
        for c in halos[1][i]:
            start(c)
        start(own_row(i))
    for r in range(HALF):
        xall[r, col] = xslot[mine[r]]

    far = CHIPS // 2

    def steps(r, dist):
        for theirs in (0, 1):
            for direction in (0, 1):
                turn = (r + theirs) % 2 == direction
                if dist == far and not turn:
                    continue
                source = lax.rem(chip + (dist if direction else -dist) + CHIPS, CHIPS)
                ring(direction, dist, r, theirs, source).wait_recv()
                if dist < far - 1 or (dist == far - 1 and turn):
                    start(ring(direction, dist + 1, r, theirs, source))

    for r in range(HALF):
        steps(r, 1)
    for r in range(HALF):
        steps(r, 2)
    for r in range(R):
        for direction, c in enumerate(halos[1][r]):
            c.wait_recv()
            start(pass_on(direction, r))

    def windows(r):
        at = pl.ds(mine[r], BAND)
        lefts[r] = jnp.concatenate(
            [
                stacked(rows_of(jnp.concatenate([win[mine_rel[r][s], at] for win in (xwin, xwin_other)], 0)))
                for s in range(K)
            ],
            1,
        )

    def p_copies(r):
        i = mine[r]
        ahead, back = R + HALF + r + 1, 2 * R - r
        copies = []
        for theirs, (n, p) in enumerate(((nxt, prv), (nxt_other, prv_other))):
            src = pother.at[r] if theirs else pwin.at[R + i]
            copies.append(
                copy(
                    src.at[pl.ds(R, ahead)], pwin.at[i, pl.ds(0, ahead)],
                    p_send.at[r, theirs, 0], p_recv.at[0, i], n,
                )
            )
            copies.append(
                copy(
                    src.at[pl.ds(r, back)], pwin.at[2 * R + i, pl.ds(R + r, back)],
                    p_send.at[r, theirs, 1], p_recv.at[1, i], p,
                )
            )
        ref = pl.ds(i, BAND)
        copies.append(
            copy(pother.at[r, ref], pwin.at[R + i, ref], p_send.at[r, 2, 0], p_give_recv.at[r], other)
        )
        return copies

    steps(0, 3)
    steps(1, 3)
    for r in range(R):
        own_row(r).wait_recv()
        for direction in (0, 1):
            pass_on(direction, r).wait_recv()
    windows(0)
    windows(1)
    for r in range(HALF):
        steps(r, 4)
        i = mine[r]
        rhs = []
        for s in range(K):
            hi, lo = split(rows_of(xall[r, :, s]))
            rhs.append(jnp.concatenate([hi, lo], 1).astype(BF16))
        square = quadrants(dot(lefts[r], jnp.concatenate(rhs, 0), 0))
        for d in range(BAND):
            s0, s1 = (square[C * e : C * e + C] * mine_keep[r][d] for e in (d, BAND + d))
            pwin[R + i, i + d] = 2.0 * xwin[R + i, i + d] - s0
            pother[r, i + d] = 2.0 * xwin_other[R + i, i + d] - s1
        for c in p_copies(r):
            start(c)

    for r in range(R):
        ahead, back = R + HALF + r % HALF + 1, 2 * R - r % HALF
        ref = pwin.at[r, pl.ds(0, ahead)]
        copy(ref, ref, p_send.at[0, 0, 0], p_recv.at[0, r], nxt).wait_recv()
        ref = pwin.at[2 * R + r, pl.ds(R + r % HALF, back)]
        copy(ref, ref, p_send.at[0, 0, 1], p_recv.at[1, r], prv).wait_recv()
    for r in range(HALF):
        i = (1 - core) * HALF + r
        ref = pwin.at[R + i, pl.ds(i, BAND)]
        copy(ref, ref, p_send.at[r, 2, 0], p_give_recv.at[r], other).wait_recv()

    for i in range(R):
        lhs = jnp.concatenate([stacked(rows_of(pwin[rrel[i][s], i : i + BAND])) for s in range(K)], 1)
        rhs = jnp.concatenate(
            [jnp.concatenate([zsplit[i, s, :, :N], zsplit[i, s, :, N:]], 0) for s in range(K)], 1
        )
        y = quadrants(dot(lhs, rhs, 1))
        for d in range(BAND):
            yband[i, i + d] = y[C * d : C * d + C]
        for t in range(K):
            out[i, t] = yband[i, frel[i][t]]

    for c in sent:
        c.wait_send()


def shards(hamiltonian, intersection_root, ham_pattern, root_pattern, filter_pattern):

    total_rows = ham_pattern.shape[0]
    hbm = pl.BlockSpec(memory_space=pltpu.HBM)
    dma = pltpu.SemaphoreType.DMA
    window = pltpu.VMEM((WIN + 1, WIN + 1, C, N), F32)
    return pl.pallas_call(
        functools.partial(kernel, total_rows),
        out_shape=jax.ShapeDtypeStruct((R, K, C, N), F32),
        in_specs=[hbm] * 5,
        out_specs=pl.BlockSpec(memory_space=pltpu.VMEM),
        scratch_shapes=[
            *[pltpu.SMEM((K, total_rows), jnp.int32)] * 3,
            pltpu.VMEM((R, K, N, N), F32),
            pltpu.VMEM((R, K, N, N), F32),
            pltpu.VMEM((R, K, 2 * N, N), BF16),
            pltpu.VMEM((R, K + 1, N, 2 * N), BF16),
            pltpu.VMEM((R // 2, N, N), F32),
            pltpu.VMEM((R, K + 1, C, N), F32),
            window,
            pltpu.VMEM((R, WIN, C, N), F32),
            pltpu.VMEM((WIN, WIN, C, N), F32),
            pltpu.VMEM((R, WIN, C, N), F32),
            pltpu.VMEM((R, WIN, C, N), F32),
            window,
            window,
            pltpu.VMEM((R, WIN + 1, C, N), F32),
            pltpu.VMEM((R, K, C, N), F32),
            pltpu.VMEM((HALF, 2 * CHIPS, K, C, N), F32),
            pltpu.VMEM((HALF, 4 * BAND * C, K * N), BF16),
            window,
            pltpu.VMEM((HALF, WIN, C, N), F32),
            pltpu.VMEM((R, WIN + 1, C, N), F32),
            dma((2, R)),
            dma((3,)),
            *[dma((2, 2, R))] * 2,
            *[dma((2 * R,))] * 2,
            *[dma((2, CHIPS // 2, 2 * HALF))] * 2,
            *[dma((HALF,))] * 2,
            *[dma((R,))] * 2,
            *[dma((2, R))] * 2,
            dma((HALF, 3, 2)),
            dma((2, R)),
            dma((HALF,)),
        ],
        compiler_params=pltpu.CompilerParams(
            collective_id=0, has_side_effects=True, vmem_limit_bytes=63 * 2**20
        ),
        cost_estimate=pl.CostEstimate(flops=4 * 270_000_000, bytes_accessed=4_400_000, transcendentals=0),
    )(hamiltonian, intersection_root, ham_pattern.T, root_pattern.T, filter_pattern.T)


def solution(mesh):
    return jax.shard_map(
        shards,
        mesh=mesh,
        in_specs=(P("rows", None, None, None), P("rows", None, None, None), P(), P(), P()),
        out_specs=P("rows", None, "cols", None),
        check_vma=False,
    )
```

```python
import functools

import jax
import jax.numpy as jnp
from jax import lax
from jax.experimental import pallas as pl
from jax.experimental.pallas import tpu as pltpu
from jax.sharding import PartitionSpec as P

R = 4
K = 8
N = 128
C = 8
BAND = 2 * R + 1
WIN = 3 * R
CHIPS = 8
HALF = R // 2
F32, BF16 = jnp.float32, jnp.bfloat16


def split(x):
    hi = x.astype(BF16).astype(F32)
    return hi, x - hi


def stacked(x):
    return jnp.concatenate(split(x), 0).astype(BF16)


def rows_of(tiles):
    return tiles.reshape(tiles.shape[0] * C, N)


def quadrants(x):
    half = x.shape[0] // 2
    return (x[half:, N:] + x[half:, :N]) + (x[:half, N:] + x[:half, :N])


def dot(a, b, b_dim):
    return lax.dot_general(a, b, (((1,), (b_dim,)), ((), ())), preferred_element_type=F32)


def kernel(
    total_rows, h_hbm, z_hbm, hp_hbm, rp_hbm, fp_hbm, out,
    hp, rp, fp, zbuf, hbuf, hsplit, zsplit, merged, zslot, zwin, wband, part, from_next, from_prev,
    xwin, xwin_other, xband, xslot, xall, lefts, pwin, pother, yband,
    load_sem, pat_sem, halo_send, halo_recv, part_send, part_recv, ring_send, ring_recv,
    give_send, give_recv, own_send, own_recv, pass_send, pass_recv, p_send, p_recv, p_give_recv,
):
    groups = total_rows // R
    row, col = lax.axis_index("rows"), lax.axis_index("cols")
    chip, core = col // 2, lax.rem(col, 2)
    mate = chip * 2 + (1 - core)
    first = row * R
    up, down = lax.rem(row + 1, groups), lax.rem(row + groups - 1, groups)
    nxt, prv = {"rows": up, "cols": col}, {"rows": down, "cols": col}
    nxt_other, prv_other = {"rows": up, "cols": mate}, {"rows": down, "cols": mate}
    right = {"rows": row, "cols": lax.rem(chip + 1, CHIPS) * 2 + core}
    left = {"rows": row, "cols": lax.rem(chip + CHIPS - 1, CHIPS) * 2 + core}
    right2 = {"rows": row, "cols": lax.rem(chip + 2, CHIPS) * 2 + core}
    left2 = {"rows": row, "cols": lax.rem(chip + CHIPS - 2, CHIPS) * 2 + core}
    other = {"rows": row, "cols": mate}

    pats = [
        pltpu.make_async_copy(a, b, pat_sem.at[i])
        for i, (a, b) in enumerate(((rp_hbm, rp), (hp_hbm, hp), (fp_hbm, fp)))
    ]
    zloads = [pltpu.make_async_copy(z_hbm.at[k], zbuf.at[k], load_sem.at[0, k]) for k in range(R)]
    hloads = [pltpu.make_async_copy(h_hbm.at[k], hbuf.at[k], load_sem.at[1, k]) for k in range(R)]
    for c in pats + zloads + hloads:
        c.start()

    for win in (zwin, xwin, xwin_other, pwin):
        for r in range(WIN + 1):
            win[r] = jnp.zeros((WIN + 1, C, N), F32)
    for k in range(R):
        wband[k] = jnp.zeros((WIN, C, N), F32)
        yband[k] = jnp.zeros((WIN + 1, C, N), F32)
        xband[k, WIN] = jnp.zeros((C, N), F32)
        zslot[k, K] = jnp.zeros((C, N), F32)
        zsplit[k, K] = jnp.zeros((N, 2 * N), BF16)
    for r in range(HALF):
        pother[r] = jnp.zeros((WIN, C, N), F32)

    barrier = pltpu.get_barrier_semaphore()
    neighbours = (nxt, prv, right, left, right2, left2, other, nxt_other, prv_other)
    for device in neighbours:
        pl.semaphore_signal(barrier, inc=1, device_id=device, device_id_type=pl.DeviceIdType.MESH)

    for c in pats:
        c.wait()

    def relative(pat, i, s):
        p = pat[s, first + i]
        v = p - first + R
        v = jnp.where(v < 0, v + total_rows, v)
        v = jnp.where(v >= total_rows, v - total_rows, v)
        return jnp.where(p < 0, WIN, jnp.minimum(v, WIN))

    def slot_at(rel, i, d):
        slot = jnp.int32(K)
        for s in range(K):
            slot = jnp.where(rel[s] == i + d, s, slot)
        return slot

    def kept(rel, i):
        return [(slot_at(rel, i, d) < K).astype(F32) for d in range(BAND)]

    rrel = [[relative(rp, i, s) for s in range(K)] for i in range(R)]
    zslots = [[slot_at(rrel[i], i, d) for d in range(BAND)] for i in range(R)]

    def copy(src, dst, send, recv, device):
        return pltpu.make_async_remote_copy(
            src_ref=src, dst_ref=dst, send_sem=send, recv_sem=recv, device_id=device,
            device_id_type=pl.DeviceIdType.MESH,
        )

    sent = []

    def start(c):
        c.start()
        sent.append(c)

    def halo(win, stage, r):
        ahead = copy(
            win.at[R + r, pl.ds(R, r + R + 1)], win.at[r, pl.ds(0, r + R + 1)],
            halo_send.at[stage, 0, r], halo_recv.at[stage, 0, r], nxt,
        )
        back = copy(
            win.at[R + r, pl.ds(r, 2 * R - r)], win.at[2 * R + r, pl.ds(r + R, 2 * R - r)],
            halo_send.at[stage, 1, r], halo_recv.at[stage, 1, r], prv,
        )
        return ahead, back

    halos = [[halo(win, stage, r) for r in range(R)] for stage, win in enumerate((zwin, xwin))]

    lane = lax.broadcasted_iota(jnp.int32, (N, N), 1) // C
    for pair in range(R // 2):
        rows = (2 * pair, 2 * pair + 1)
        for k in rows:
            zloads[k].wait()
        m = jnp.zeros((N, N), F32)
        for q in range(2 * K):
            v = zbuf[2 * pair + q // K, q % K]
            v = jnp.where(lane == col, v, 0.0)
            m += pltpu.roll(v, q * C, 1) if q else v
        merged[pair] = m.T
        for q in range(2 * K):
            at = pl.multiple_of(lax.rem(col + q, 2 * K) * C, C)
            zslot[2 * pair + q // K, q % K] = merged[pair, pl.ds(at, C), :]
        for k in rows:
            for d in range(BAND):
                zwin[R + k, k + d] = zslot[k, zslots[k][d]]
        if pair == 0:
            pl.semaphore_wait(barrier, len(neighbours))
        for k in rows:
            for c in halos[0][k]:
                start(c)

    hrel = [[relative(hp, i, s) for s in range(K)] for i in range(R)]
    frel = [[relative(fp, i, s) for s in range(K)] for i in range(R)]
    keep = [kept(frel[i], i) for i in range(R)]
    mine = [core * HALF + r for r in range(HALF)]
    mine_rel = [[relative(fp, i, s) for s in range(K)] for i in mine]
    mine_keep = [kept(rel, i) for rel, i in zip(mine_rel, mine)]
    for k in range(R):
        for s in range(K):
            hi, lo = split(zbuf[k, s])
            zsplit[k, s] = jnp.concatenate([hi, lo], 1).astype(BF16)
    for k in range(R):
        hloads[k].wait()
        for s in range(K):
            hsplit[k, s] = stacked(hbuf[k, s])
    for r in range(R):
        for c in halos[0][r]:
            c.wait_recv()

    for i in range(R):
        lhs = jnp.concatenate([stacked(rows_of(zwin[hrel[i][s], i : i + BAND])) for s in range(K)], 1)
        rhs = jnp.concatenate([hsplit[i, s] for s in range(K)], 1)
        w = quadrants(dot(lhs, rhs, 1))
        for d in range(BAND):
            wband[i, i + d] = w[C * d : C * d + C] * keep[i][d]

    def part_copy(w):
        if w < R:
            n = w + R + 1
            return copy(
                part.at[w, pl.ds(0, n)], from_next.at[w, pl.ds(R, n)], part_send.at[w], part_recv.at[w], prv
            )
        r = w - 2 * R
        n = 2 * R - r
        return copy(
            part.at[w, pl.ds(r + R, n)], from_prev.at[r, pl.ds(r, n)], part_send.at[r + R], part_recv.at[r + R], nxt
        )

    parts = {w: part_copy(w) for w in (*range(R), *range(2 * R, 3 * R))}
    order = [w for r in range(R) for w in (r, 2 * R + r)] + list(range(R, 2 * R))
    for w in order:
        ks = [k for k in range(R) if 0 <= w - k < BAND]
        lo, hi = max(0, w - R), min(WIN, w + R + 1)
        lhs = jnp.concatenate([stacked(rows_of(wband[k, lo:hi])) for k in ks], 1)
        rhs = jnp.concatenate([zsplit[k, zslots[k][w - k]] for k in ks], 0)
        x = quadrants(dot(lhs, rhs, 0))
        for j in range(lo, hi):
            part[w, j] = x[C * (j - lo) : C * (j - lo) + C]
        if w in parts:
            start(parts[w])

    far = CHIPS // 2

    def ring(direction, dist, r, theirs, source, src=None):
        ref = xall.at[r, source * 2 + (1 - core if theirs else core)]
        piece = 2 * r + theirs
        return copy(
            ref if src is None else src, ref, ring_send.at[direction, dist - 1, piece],
            ring_recv.at[direction, dist - 1, piece], (left2, right2, left, right)[2 * (dist % 2) + (not direction)],
        )

    def give(r):
        return copy(xslot.at[(1 - core) * HALF + r], xall.at[r, col], give_send.at[r], give_recv.at[r], other)

    def given(r):
        return copy(xslot.at[r], xall.at[r, mate], give_send.at[r], give_recv.at[r], other)

    for i in range(R):
        parts[i].wait_recv()
        parts[2 * R + i].wait_recv()
        for d in range(BAND):
            j = i + d
            x = part[R + i, j]
            if j >= R:
                x += from_next[i, j]
            if j < 2 * R:
                x += from_prev[i, j]
            x *= keep[i][d]
            xwin[R + i, j] = x
            xband[i, j] = x
        for t in range(K):
            xslot[i, t] = xband[i, frel[i][t]]

        @pl.when(core == i // HALF)
        def _():
            for dist in (2, 1):
                for direction in (0, 1):
                    ring(direction, dist, i % HALF, 0, chip, xslot.at[i]).start()

        @pl.when(core != i // HALF)
        def _():
            give(i % HALF).start()

        if i % HALF == HALF - 1 and i > HALF:
            for r in range(HALF):
                given(r).wait_recv()
                for dist in (2, 1):
                    for direction in (0, 1):
                        start(ring(direction, dist, r, 1, chip))

    for r in range(HALF):
        sent += [give(r)] + [ring(direction, dist, r, 0, chip, xslot.at[r]) for direction in (0, 1) for dist in (1, 2)]

    def own_row(i):
        ref = (R + i, pl.ds(i, BAND))
        return copy(xwin.at[ref], xwin_other.at[ref], own_send.at[i], own_recv.at[i], other)

    def pass_on(direction, r):
        ref = (r, pl.ds(0, r + R + 1)) if direction == 0 else (2 * R + r, pl.ds(r + R, 2 * R - r))
        return copy(xwin.at[ref], xwin_other.at[ref], pass_send.at[direction, r], pass_recv.at[direction, r], other)

    for i in range(R):
        for c in halos[1][i]:
            start(c)
        start(own_row(i))
    for r in range(HALF):
        xall[r, col] = xslot[mine[r]]

    def steps(r, dist):
        for theirs in (0, 1):
            for direction in (0, 1):
                turn = (r + theirs) % 2 == direction
                if dist == far and not turn:
                    continue
                source = lax.rem(chip + (dist if direction else -dist) + CHIPS, CHIPS)
                ring(direction, dist, r, theirs, source).wait_recv()
                if dist == 2:
                    if turn:
                        start(ring(direction, far, r, theirs, source))
                    start(ring(direction, 3, r, theirs, source))

    for r in range(HALF):
        steps(r, 2)
    for r in range(HALF):
        steps(r, 1)
    for r in range(R):
        for direction, c in enumerate(halos[1][r]):
            c.wait_recv()
            start(pass_on(direction, r))

    def windows(r):
        at = pl.ds(mine[r], BAND)
        lefts[r] = jnp.concatenate(
            [
                stacked(rows_of(jnp.concatenate([win[mine_rel[r][s], at] for win in (xwin, xwin_other)], 0)))
                for s in range(K)
            ],
            1,
        )

    def p_copies(r):
        i = mine[r]
        ahead, back = R + HALF + r + 1, 2 * R - r
        copies = []
        for theirs, (n, p) in enumerate(((nxt, prv), (nxt_other, prv_other))):
            src = pother.at[r] if theirs else pwin.at[R + i]
            copies.append(
                copy(
                    src.at[pl.ds(R, ahead)], pwin.at[i, pl.ds(0, ahead)],
                    p_send.at[r, theirs, 0], p_recv.at[0, i], n,
                )
            )
            copies.append(
                copy(
                    src.at[pl.ds(r, back)], pwin.at[2 * R + i, pl.ds(R + r, back)],
                    p_send.at[r, theirs, 1], p_recv.at[1, i], p,
                )
            )
        ref = pl.ds(i, BAND)
        copies.append(
            copy(pother.at[r, ref], pwin.at[R + i, ref], p_send.at[r, 2, 0], p_give_recv.at[r], other)
        )
        return copies

    steps(0, 3)
    steps(1, 3)
    for r in range(R):
        own_row(r).wait_recv()
        for direction in (0, 1):
            pass_on(direction, r).wait_recv()
    windows(0)
    windows(1)
    for r in range(HALF):
        steps(r, 4)
        i = mine[r]
        rhs = []
        for s in range(K):
            hi, lo = split(rows_of(xall[r, :, s]))
            rhs.append(jnp.concatenate([hi, lo], 1).astype(BF16))
        square = quadrants(dot(lefts[r], jnp.concatenate(rhs, 0), 0))
        for d in range(BAND):
            s0, s1 = (square[C * e : C * e + C] * mine_keep[r][d] for e in (d, BAND + d))
            pwin[R + i, i + d] = 2.0 * xwin[R + i, i + d] - s0
            pother[r, i + d] = 2.0 * xwin_other[R + i, i + d] - s1
        for c in p_copies(r):
            start(c)

    for r in range(R):
        ahead, back = R + HALF + r % HALF + 1, 2 * R - r % HALF
        ref = pwin.at[r, pl.ds(0, ahead)]
        copy(ref, ref, p_send.at[0, 0, 0], p_recv.at[0, r], nxt).wait_recv()
        ref = pwin.at[2 * R + r, pl.ds(R + r % HALF, back)]
        copy(ref, ref, p_send.at[0, 0, 1], p_recv.at[1, r], prv).wait_recv()
    for r in range(HALF):
        i = (1 - core) * HALF + r
        ref = pwin.at[R + i, pl.ds(i, BAND)]
        copy(ref, ref, p_send.at[r, 2, 0], p_give_recv.at[r], other).wait_recv()

    for i in range(R):
        lhs = jnp.concatenate([stacked(rows_of(pwin[rrel[i][s], i : i + BAND])) for s in range(K)], 1)
        rhs = jnp.concatenate(
            [jnp.concatenate([zsplit[i, s, :, :N], zsplit[i, s, :, N:]], 0) for s in range(K)], 1
        )
        y = quadrants(dot(lhs, rhs, 1))
        for d in range(BAND):
            yband[i, i + d] = y[C * d : C * d + C]
        for t in range(K):
            out[i, t] = yband[i, frel[i][t]]

    for c in sent:
        c.wait_send()


def shards(hamiltonian, intersection_root, ham_pattern, root_pattern, filter_pattern):

    total_rows = ham_pattern.shape[0]
    hbm = pl.BlockSpec(memory_space=pltpu.HBM)
    dma = pltpu.SemaphoreType.DMA
    window = pltpu.VMEM((WIN + 1, WIN + 1, C, N), F32)
    return pl.pallas_call(
        functools.partial(kernel, total_rows),
        out_shape=jax.ShapeDtypeStruct((R, K, C, N), F32),
        in_specs=[hbm] * 5,
        out_specs=pl.BlockSpec(memory_space=pltpu.VMEM),
        scratch_shapes=[
            *[pltpu.SMEM((K, total_rows), jnp.int32)] * 3,
            pltpu.VMEM((R, K, N, N), F32),
            pltpu.VMEM((R, K, N, N), F32),
            pltpu.VMEM((R, K, 2 * N, N), BF16),
            pltpu.VMEM((R, K + 1, N, 2 * N), BF16),
            pltpu.VMEM((R // 2, N, N), F32),
            pltpu.VMEM((R, K + 1, C, N), F32),
            window,
            pltpu.VMEM((R, WIN, C, N), F32),
            pltpu.VMEM((WIN, WIN, C, N), F32),
            pltpu.VMEM((R, WIN, C, N), F32),
            pltpu.VMEM((R, WIN, C, N), F32),
            window,
            window,
            pltpu.VMEM((R, WIN + 1, C, N), F32),
            pltpu.VMEM((R, K, C, N), F32),
            pltpu.VMEM((HALF, 2 * CHIPS, K, C, N), F32),
            pltpu.VMEM((HALF, 4 * BAND * C, K * N), BF16),
            window,
            pltpu.VMEM((HALF, WIN, C, N), F32),
            pltpu.VMEM((R, WIN + 1, C, N), F32),
            dma((2, R)),
            dma((3,)),
            *[dma((2, 2, R))] * 2,
            *[dma((2 * R,))] * 2,
            *[dma((2, CHIPS // 2, 2 * HALF))] * 2,
            *[dma((HALF,))] * 2,
            *[dma((R,))] * 2,
            *[dma((2, R))] * 2,
            dma((HALF, 3, 2)),
            dma((2, R)),
            dma((HALF,)),
        ],
        compiler_params=pltpu.CompilerParams(
            collective_id=0, has_side_effects=True, vmem_limit_bytes=63 * 2**20
        ),
        cost_estimate=pl.CostEstimate(flops=4 * 270_000_000, bytes_accessed=4_400_000, transcendentals=0),
    )(hamiltonian, intersection_root, ham_pattern.T, root_pattern.T, filter_pattern.T)


def solution(mesh):
    return jax.shard_map(
        shards,
        mesh=mesh,
        in_specs=(P("rows", None, None, None), P("rows", None, None, None), P(), P(), P()),
        out_specs=P("rows", None, "cols", None),
        check_vma=False,
    )
```

```python
import functools

import jax
import jax.numpy as jnp
from jax import lax
from jax.experimental import pallas as pl
from jax.experimental.pallas import tpu as pltpu
from jax.sharding import PartitionSpec as P

R = 4
K = 8
N = 128
C = 8
BAND = 2 * R + 1
WIN = 3 * R
CHIPS = 8
HALF = R // 2
F32, BF16 = jnp.float32, jnp.bfloat16


def split(x):
    hi = x.astype(BF16).astype(F32)
    return hi, x - hi


def stacked(x):
    return jnp.concatenate(split(x), 0).astype(BF16)


def rows_of(tiles):
    return tiles.reshape(tiles.shape[0] * C, N)


def quadrants(x):
    half = x.shape[0] // 2
    return (x[half:, N:] + x[half:, :N]) + (x[:half, N:] + x[:half, :N])


def dot(a, b, b_dim):
    return lax.dot_general(a, b, (((1,), (b_dim,)), ((), ())), preferred_element_type=F32)


def kernel(
    total_rows, h_hbm, z_hbm, hp_hbm, rp_hbm, fp_hbm, out,
    hp, rp, fp, zbuf, hbuf, hsplit, zsplit, merged, zslot, zwin, wband, part, from_next, from_prev,
    xwin, xwin_other, xband, xslot, xall, lefts, pwin, pother, yband,
    load_sem, pat_sem, halo_send, halo_recv, part_send, part_recv, ring_send, ring_recv,
    give_send, give_recv, own_send, own_recv, pass_send, pass_recv, p_send, p_recv, p_give_recv,
):
    groups = total_rows // R
    row, col = lax.axis_index("rows"), lax.axis_index("cols")
    chip, core = col // 2, lax.rem(col, 2)
    mate = chip * 2 + (1 - core)
    first = row * R
    up, down = lax.rem(row + 1, groups), lax.rem(row + groups - 1, groups)
    nxt, prv = {"rows": up, "cols": col}, {"rows": down, "cols": col}
    nxt_other, prv_other = {"rows": up, "cols": mate}, {"rows": down, "cols": mate}
    right = {"rows": row, "cols": lax.rem(chip + 1, CHIPS) * 2 + core}
    left = {"rows": row, "cols": lax.rem(chip + CHIPS - 1, CHIPS) * 2 + core}
    right2 = {"rows": row, "cols": lax.rem(chip + 2, CHIPS) * 2 + core}
    left2 = {"rows": row, "cols": lax.rem(chip + CHIPS - 2, CHIPS) * 2 + core}
    other = {"rows": row, "cols": mate}

    pats = [
        pltpu.make_async_copy(a, b, pat_sem.at[i])
        for i, (a, b) in enumerate(((rp_hbm, rp), (hp_hbm, hp), (fp_hbm, fp)))
    ]
    zloads = [pltpu.make_async_copy(z_hbm.at[k], zbuf.at[k], load_sem.at[0, k]) for k in range(R)]
    hloads = [pltpu.make_async_copy(h_hbm.at[k], hbuf.at[k], load_sem.at[1, k]) for k in range(R)]
    for c in pats + zloads:
        c.start()

    for win in (zwin, xwin, xwin_other, pwin):
        for r in range(WIN + 1):
            win[r] = jnp.zeros((WIN + 1, C, N), F32)
    for k in range(R):
        wband[k] = jnp.zeros((WIN, C, N), F32)
        yband[k] = jnp.zeros((WIN + 1, C, N), F32)
        xband[k, WIN] = jnp.zeros((C, N), F32)
        zslot[k, K] = jnp.zeros((C, N), F32)
        zsplit[k, K] = jnp.zeros((N, 2 * N), BF16)
    for r in range(HALF):
        pother[r] = jnp.zeros((WIN, C, N), F32)

    barrier = pltpu.get_barrier_semaphore()
    neighbours = (nxt, prv, right, left, right2, left2, other, nxt_other, prv_other)
    for device in neighbours:
        pl.semaphore_signal(barrier, inc=1, device_id=device, device_id_type=pl.DeviceIdType.MESH)

    for c in pats:
        c.wait()

    def relative(pat, i, s):
        p = pat[s, first + i]
        v = p - first + R
        v = jnp.where(v < 0, v + total_rows, v)
        v = jnp.where(v >= total_rows, v - total_rows, v)
        return jnp.where(p < 0, WIN, jnp.minimum(v, WIN))

    def slot_at(rel, i, d):
        slot = jnp.int32(K)
        for s in range(K):
            slot = jnp.where(rel[s] == i + d, s, slot)
        return slot

    def kept(rel, i):
        return [(slot_at(rel, i, d) < K).astype(F32) for d in range(BAND)]

    rrel = [[relative(rp, i, s) for s in range(K)] for i in range(R)]
    zslots = [[slot_at(rrel[i], i, d) for d in range(BAND)] for i in range(R)]

    def copy(src, dst, send, recv, device):
        return pltpu.make_async_remote_copy(
            src_ref=src, dst_ref=dst, send_sem=send, recv_sem=recv, device_id=device,
            device_id_type=pl.DeviceIdType.MESH,
        )

    sent = []

    def start(c):
        c.start()
        sent.append(c)

    def halo(win, stage, r):
        ahead = copy(
            win.at[R + r, pl.ds(R, r + R + 1)], win.at[r, pl.ds(0, r + R + 1)],
            halo_send.at[stage, 0, r], halo_recv.at[stage, 0, r], nxt,
        )
        back = copy(
            win.at[R + r, pl.ds(r, 2 * R - r)], win.at[2 * R + r, pl.ds(r + R, 2 * R - r)],
            halo_send.at[stage, 1, r], halo_recv.at[stage, 1, r], prv,
        )
        return ahead, back

    halos = [[halo(win, stage, r) for r in range(R)] for stage, win in enumerate((zwin, xwin))]

    lane = lax.broadcasted_iota(jnp.int32, (N, N), 1) // C
    for pair in range(R // 2):
        rows = (2 * pair, 2 * pair + 1)
        for k in rows:
            zloads[k].wait()
        if pair == R // 2 - 1:
            for c in hloads:
                c.start()
        m = jnp.zeros((N, N), F32)
        for q in range(2 * K):
            v = zbuf[2 * pair + q // K, q % K]
            v = jnp.where(lane == col, v, 0.0)
            m += pltpu.roll(v, q * C, 1) if q else v
        merged[pair] = m.T
        for q in range(2 * K):
            at = pl.multiple_of(lax.rem(col + q, 2 * K) * C, C)
            zslot[2 * pair + q // K, q % K] = merged[pair, pl.ds(at, C), :]
        for k in rows:
            for d in range(BAND):
                zwin[R + k, k + d] = zslot[k, zslots[k][d]]
        if pair == 0:
            pl.semaphore_wait(barrier, len(neighbours))
        for k in rows:
            for c in halos[0][k]:
                start(c)

    hrel = [[relative(hp, i, s) for s in range(K)] for i in range(R)]
    frel = [[relative(fp, i, s) for s in range(K)] for i in range(R)]
    keep = [kept(frel[i], i) for i in range(R)]
    mine = [core * HALF + r for r in range(HALF)]
    mine_rel = [[relative(fp, i, s) for s in range(K)] for i in mine]
    mine_keep = [kept(rel, i) for rel, i in zip(mine_rel, mine)]
    for k in range(R):
        for s in range(K):
            hi, lo = split(zbuf[k, s])
            zsplit[k, s] = jnp.concatenate([hi, lo], 1).astype(BF16)
    for k in range(R):
        hloads[k].wait()
        for s in range(K):
            hsplit[k, s] = stacked(hbuf[k, s])
    for r in range(R):
        for c in halos[0][r]:
            c.wait_recv()

    for i in range(R):
        lhs = jnp.concatenate([stacked(rows_of(zwin[hrel[i][s], i : i + BAND])) for s in range(K)], 1)
        rhs = jnp.concatenate([hsplit[i, s] for s in range(K)], 1)
        w = quadrants(dot(lhs, rhs, 1))
        for d in range(BAND):
            wband[i, i + d] = w[C * d : C * d + C] * keep[i][d]

    def part_copy(w):
        if w < R:
            n = w + R + 1
            return copy(
                part.at[w, pl.ds(0, n)], from_next.at[w, pl.ds(R, n)], part_send.at[w], part_recv.at[w], prv
            )
        r = w - 2 * R
        n = 2 * R - r
        return copy(
            part.at[w, pl.ds(r + R, n)], from_prev.at[r, pl.ds(r, n)], part_send.at[r + R], part_recv.at[r + R], nxt
        )

    parts = {w: part_copy(w) for w in (*range(R), *range(2 * R, 3 * R))}
    order = [w for r in range(R) for w in (r, 2 * R + r)] + list(range(R, 2 * R))
    for w in order:
        ks = [k for k in range(R) if 0 <= w - k < BAND]
        lo, hi = max(0, w - R), min(WIN, w + R + 1)
        lhs = jnp.concatenate([stacked(rows_of(wband[k, lo:hi])) for k in ks], 1)
        rhs = jnp.concatenate([zsplit[k, zslots[k][w - k]] for k in ks], 0)
        x = quadrants(dot(lhs, rhs, 0))
        for j in range(lo, hi):
            part[w, j] = x[C * (j - lo) : C * (j - lo) + C]
        if w in parts:
            start(parts[w])

    far = CHIPS // 2

    def ring(direction, dist, r, theirs, source, src=None):
        ref = xall.at[r, source * 2 + (1 - core if theirs else core)]
        piece = 2 * r + theirs
        return copy(
            ref if src is None else src, ref, ring_send.at[direction, dist - 1, piece],
            ring_recv.at[direction, dist - 1, piece], (left2, right2, left, right)[2 * (dist % 2) + (not direction)],
        )

    def give(r):
        return copy(xslot.at[(1 - core) * HALF + r], xall.at[r, col], give_send.at[r], give_recv.at[r], other)

    def given(r):
        return copy(xslot.at[r], xall.at[r, mate], give_send.at[r], give_recv.at[r], other)

    for i in range(R):
        parts[i].wait_recv()
        parts[2 * R + i].wait_recv()
        for d in range(BAND):
            j = i + d
            x = part[R + i, j]
            if j >= R:
                x += from_next[i, j]
            if j < 2 * R:
                x += from_prev[i, j]
            x *= keep[i][d]
            xwin[R + i, j] = x
            xband[i, j] = x
        for t in range(K):
            xslot[i, t] = xband[i, frel[i][t]]

        @pl.when(core == i // HALF)
        def _():
            for dist in (2, 1):
                for direction in (0, 1):
                    ring(direction, dist, i % HALF, 0, chip, xslot.at[i]).start()

        @pl.when(core != i // HALF)
        def _():
            give(i % HALF).start()

        if i % HALF == HALF - 1 and i > HALF:
            for r in range(HALF):
                given(r).wait_recv()
                for dist in (2, 1):
                    for direction in (0, 1):
                        start(ring(direction, dist, r, 1, chip))

    for r in range(HALF):
        sent += [give(r)] + [ring(direction, dist, r, 0, chip, xslot.at[r]) for direction in (0, 1) for dist in (1, 2)]

    def own_row(i):
        ref = (R + i, pl.ds(i, BAND))
        return copy(xwin.at[ref], xwin_other.at[ref], own_send.at[i], own_recv.at[i], other)

    def pass_on(direction, r):
        ref = (r, pl.ds(0, r + R + 1)) if direction == 0 else (2 * R + r, pl.ds(r + R, 2 * R - r))
        return copy(xwin.at[ref], xwin_other.at[ref], pass_send.at[direction, r], pass_recv.at[direction, r], other)

    for i in range(R):
        for c in halos[1][i]:
            start(c)
        start(own_row(i))
    for r in range(HALF):
        xall[r, col] = xslot[mine[r]]

    def steps(r, dist):
        for theirs in (0, 1):
            for direction in (0, 1):
                turn = (r + theirs) % 2 == direction
                if dist == far and not turn:
                    continue
                source = lax.rem(chip + (dist if direction else -dist) + CHIPS, CHIPS)
                ring(direction, dist, r, theirs, source).wait_recv()
                if dist == 2:
                    if turn:
                        start(ring(direction, far, r, theirs, source))
                    start(ring(direction, 3, r, theirs, source))

    for r in range(HALF):
        steps(r, 2)
    for r in range(HALF):
        steps(r, 1)
    for r in range(R):
        for direction, c in enumerate(halos[1][r]):
            c.wait_recv()
            start(pass_on(direction, r))

    def windows(r):
        at = pl.ds(mine[r], BAND)
        lefts[r] = jnp.concatenate(
            [
                stacked(rows_of(jnp.concatenate([win[mine_rel[r][s], at] for win in (xwin, xwin_other)], 0)))
                for s in range(K)
            ],
            1,
        )

    def p_copies(r):
        i = mine[r]
        ahead, back = R + HALF + r + 1, 2 * R - r
        copies = []
        for theirs, (n, p) in enumerate(((nxt, prv), (nxt_other, prv_other))):
            src = pother.at[r] if theirs else pwin.at[R + i]
            copies.append(
                copy(
                    src.at[pl.ds(R, ahead)], pwin.at[i, pl.ds(0, ahead)],
                    p_send.at[r, theirs, 0], p_recv.at[0, i], n,
                )
            )
            copies.append(
                copy(
                    src.at[pl.ds(r, back)], pwin.at[2 * R + i, pl.ds(R + r, back)],
                    p_send.at[r, theirs, 1], p_recv.at[1, i], p,
                )
            )
        ref = pl.ds(i, BAND)
        copies.append(
            copy(pother.at[r, ref], pwin.at[R + i, ref], p_send.at[r, 2, 0], p_give_recv.at[r], other)
        )
        return copies

    steps(0, 3)
    steps(1, 3)
    for r in range(R):
        own_row(r).wait_recv()
        for direction in (0, 1):
            pass_on(direction, r).wait_recv()
    windows(0)
    windows(1)
    for r in range(HALF):
        steps(r, 4)
        i = mine[r]
        rhs = []
        for s in range(K):
            hi, lo = split(rows_of(xall[r, :, s]))
            rhs.append(jnp.concatenate([hi, lo], 1).astype(BF16))
        square = quadrants(dot(lefts[r], jnp.concatenate(rhs, 0), 0))
        for d in range(BAND):
            s0, s1 = (square[C * e : C * e + C] * mine_keep[r][d] for e in (d, BAND + d))
            pwin[R + i, i + d] = 2.0 * xwin[R + i, i + d] - s0
            pother[r, i + d] = 2.0 * xwin_other[R + i, i + d] - s1
        for c in p_copies(r):
            start(c)

    for r in range(R):
        ahead, back = R + HALF + r % HALF + 1, 2 * R - r % HALF
        ref = pwin.at[r, pl.ds(0, ahead)]
        copy(ref, ref, p_send.at[0, 0, 0], p_recv.at[0, r], nxt).wait_recv()
        ref = pwin.at[2 * R + r, pl.ds(R + r % HALF, back)]
        copy(ref, ref, p_send.at[0, 0, 1], p_recv.at[1, r], prv).wait_recv()
    for r in range(HALF):
        i = (1 - core) * HALF + r
        ref = pwin.at[R + i, pl.ds(i, BAND)]
        copy(ref, ref, p_send.at[r, 2, 0], p_give_recv.at[r], other).wait_recv()

    for i in range(R):
        lhs = jnp.concatenate([stacked(rows_of(pwin[rrel[i][s], i : i + BAND])) for s in range(K)], 1)
        rhs = jnp.concatenate(
            [jnp.concatenate([zsplit[i, s, :, :N], zsplit[i, s, :, N:]], 0) for s in range(K)], 1
        )
        y = quadrants(dot(lhs, rhs, 1))
        for d in range(BAND):
            yband[i, i + d] = y[C * d : C * d + C]
        for t in range(K):
            out[i, t] = yband[i, frel[i][t]]

    for c in sent:
        c.wait_send()


def shards(hamiltonian, intersection_root, ham_pattern, root_pattern, filter_pattern):

    total_rows = ham_pattern.shape[0]
    hbm = pl.BlockSpec(memory_space=pltpu.HBM)
    dma = pltpu.SemaphoreType.DMA
    window = pltpu.VMEM((WIN + 1, WIN + 1, C, N), F32)
    return pl.pallas_call(
        functools.partial(kernel, total_rows),
        out_shape=jax.ShapeDtypeStruct((R, K, C, N), F32),
        in_specs=[hbm] * 5,
        out_specs=pl.BlockSpec(memory_space=pltpu.VMEM),
        scratch_shapes=[
            *[pltpu.SMEM((K, total_rows), jnp.int32)] * 3,
            pltpu.VMEM((R, K, N, N), F32),
            pltpu.VMEM((R, K, N, N), F32),
            pltpu.VMEM((R, K, 2 * N, N), BF16),
            pltpu.VMEM((R, K + 1, N, 2 * N), BF16),
            pltpu.VMEM((R // 2, N, N), F32),
            pltpu.VMEM((R, K + 1, C, N), F32),
            window,
            pltpu.VMEM((R, WIN, C, N), F32),
            pltpu.VMEM((WIN, WIN, C, N), F32),
            pltpu.VMEM((R, WIN, C, N), F32),
            pltpu.VMEM((R, WIN, C, N), F32),
            window,
            window,
            pltpu.VMEM((R, WIN + 1, C, N), F32),
            pltpu.VMEM((R, K, C, N), F32),
            pltpu.VMEM((HALF, 2 * CHIPS, K, C, N), F32),
            pltpu.VMEM((HALF, 4 * BAND * C, K * N), BF16),
            window,
            pltpu.VMEM((HALF, WIN, C, N), F32),
            pltpu.VMEM((R, WIN + 1, C, N), F32),
            dma((2, R)),
            dma((3,)),
            *[dma((2, 2, R))] * 2,
            *[dma((2 * R,))] * 2,
            *[dma((2, CHIPS // 2, 2 * HALF))] * 2,
            *[dma((HALF,))] * 2,
            *[dma((R,))] * 2,
            *[dma((2, R))] * 2,
            dma((HALF, 3, 2)),
            dma((2, R)),
            dma((HALF,)),
        ],
        compiler_params=pltpu.CompilerParams(
            collective_id=0, has_side_effects=True, vmem_limit_bytes=63 * 2**20
        ),
        cost_estimate=pl.CostEstimate(flops=4 * 270_000_000, bytes_accessed=4_400_000, transcendentals=0),
    )(hamiltonian, intersection_root, ham_pattern.T, root_pattern.T, filter_pattern.T)


def solution(mesh):
    return jax.shard_map(
        shards,
        mesh=mesh,
        in_specs=(P("rows", None, None, None), P("rows", None, None, None), P(), P(), P()),
        out_specs=P("rows", None, "cols", None),
        check_vma=False,
    )
```
